32 devices in a mesh: rx: 4 (over x, core), ry: 8 (over z, y).
Axes of the slice: x: 2, y: 2, z: 4, core: 2. Of those that a mesh axis runs over, the one named last changes fastest.
Arguments:
- panel: float32 [64, 524288], P(None, ('rx', 'ry')), may hold values from -6 to 6
- signs: int32 [524288], P(('rx', 'ry')), may hold values from -1 to 1, as said below
- sample_block: int32 [768], P(('rx', 'ry')), may hold values from 0 to 127
- sample_owner: int32 [768, 1], P(('rx', 'ry')), may hold values from 0 to 7; in each aligned block of 24 rows (0 to 23, 24 to 47, ...) at most 4 rows name the same one
Outputs:
- mixed: float32 [64, 524288], P(None, ('rx', 'ry'))
- sketch_blocks: float32 [64, 1024, 128], P(None, ('rx', 'ry'))
- r_factor: float32 [64, 64], replicated
- leverage: float32 [524288], P(('rx', 'ry'))
The draws below stay inside these ranges and needn't reach their ends.
Inputs may be any that keep to these rules, and one draw needn't show every extreme that they name: `signs`: each entry is +1 or -1. `sample_owner`: among the 24 entries of one device no owner is named more than 4 times; in every draw some device names some owner exactly 4 times.
All inputs are finite; a program needn't handle non-finite values.
Results may differ from the reference program's by a relative error of at most 0.0003.
Values sent between devices are 32-bit elements; how exact they have to be, the bound alone decides.
A program may use at most 64 MiB of HBM per device.

```python
import math
import jax
import jax.numpy as jnp
import numpy as np
from jax import lax

COLS = 64
BLOCK = 128
R_DEV = 16384
K = 24
CAP = 4
ROWS = 524288
BLK_DEV = 128
SLOTS = 32
SKETCH = 98304
N_RX = 4
N_RY = 8


def draw_signs(key, part):
    key = jax.random.fold_in(key, 11)
    coin_bits = jax.random.randint(key, (ROWS,), 0, 2, dtype=jnp.int32)
    return 2 * coin_bits - 1


def with_ends(values, key, least, top_value):
    longest = values.shape.index(max(values.shape))
    spots = []
    for shift in (0, 1):
        where = [jax.random.randint(jax.random.fold_in(key, axis), (), 0, length) for axis, length in enumerate(values.shape)]
        where[longest] = (where[longest] + shift) % values.shape[longest]
        spots.append(tuple(where))
    return values.at[spots[0]].set(least).at[spots[1]].set(top_value)


def shard_levels(own_key, dims, split, smallest, top_value):
    def one(axis_at, parts):
        steps = jax.random.uniform(jax.random.fold_in(jax.random.fold_in(own_key, 6), axis_at), (parts,), jnp.float32, smallest / len(split), top_value / len(split))
        return jnp.repeat(jnp.exp(steps), dims[axis_at] // parts).reshape((-1,) + (1,) * (len(dims) - axis_at - 1))

    level = one(*split[0])
    for cut in split[1:]:
        level = level * one(*cut)
    return level


def assign_block(key, own, number, rows, number_of, top, limit, lean):
    sequence = jax.random.permutation(key, number_of)
    packed, common = portions_of(number_of, rows * top, limit, lean, True), portions_of(number_of, rows * top, limit, lean, False)
    places = jnp.arange(number_of)

    def named(sizes, turn):
        used = int((sizes > 0).sum())
        fixed = max(1, used // 4)
        moved = fixed + (places - fixed + turn * (used - fixed)) % max(1, number_of - fixed)
        return jnp.zeros((number_of,), jnp.int32).at[sequence[jnp.where(places < fixed, places, moved)]].set(jnp.asarray(sizes, jnp.int32))

    sizes = jnp.where(number % 4 == 0, named(packed, number // 4), named(common, number - number // 4 - 1))
    mixed = jax.random.permutation(jax.random.fold_in(own, 3), number_of)
    source_of, taker = mixed[0:number_of // 2 * 2:2], mixed[1:number_of // 2 * 2:2]
    margin = jnp.minimum(sizes[source_of] - 1, limit - sizes[taker]) // 2
    margin = jnp.where((source_of == sequence[0]) | (taker == sequence[0]) | (sizes[taker] == 0), 0, jnp.maximum(margin, 0))
    moved = jax.random.randint(jax.random.fold_in(own, 4), (number_of // 2,), 0, 1 << 20) % (margin + 1)
    sizes = sizes.at[source_of].add(-moved).at[taker].add(moved)
    items = jnp.searchsorted(jnp.cumsum(sizes), jnp.arange(rows * top), side="right").astype(jnp.int32)
    table = items.reshape(top, rows).T
    table = table[jax.random.permutation(jax.random.fold_in(own, 1), rows)]
    turn = jax.random.randint(jax.random.fold_in(own, 2), (rows, 1), 0, top)
    return jnp.take_along_axis(table, (jnp.arange(top)[None, :] + turn) % top, axis=1)


def portions_of(number_of, total, most, slope, full):
    weights = [(1 << 20) // math.isqrt(standing ** slope) + 1 for standing in range(1, number_of + 1)]
    largest = most if full else min(most, max(-(-total // number_of), total * weights[0] // sum(weights)))
    least = 1 if total - largest >= number_of - 1 else 0
    holding, spare = [largest] + [least] * (number_of - 1), total - largest - least * (number_of - 1)
    while spare > 0:
        candidates = [i for i in range(1, number_of) if holding[i] < largest] or [i for i in range(1, number_of) if holding[i] < most]
        mass, budget = sum([weights[i] for i in candidates]), spare
        for i in candidates:
            addition = min(most - holding[i], max(1, budget * weights[i] // mass), spare)
            holding[i] = holding[i] + addition
            spare = spare - addition
    return np.array(holding)


def normal_values(rng, shape, width, limit, shards=(), kind=jnp.bfloat16):
    values = width * jax.random.normal(rng, shape, jnp.float32)
    if shards:
        values = values * shard_levels(rng, shape, shards, -0.22, 0.18)
    return jnp.clip(values, -limit, limit).astype(kind)


def setup_inputs(seed: int = 0) -> dict:
    seeds = jax.random.split(jax.random.key(seed), 5)
    panel = normal_values(seeds[0], (COLS, ROWS), 1.0, 6.0, ((1, 32),), jnp.float32)
    signs = draw_signs(jax.random.fold_in(seeds[4], 71), 0)
    sample_block = with_ends(jax.random.randint(seeds[2], (K * N_RX * N_RY,), 0, BLK_DEV), jax.random.fold_in(seeds[2], 1), 0, BLK_DEV - 1).astype(jnp.int32)
    sample_owner_keys = jax.random.split(jax.random.fold_in(seeds[3], 1), (K * N_RX * N_RY) // K)
    sample_owner_turns = jax.random.permutation(jax.random.fold_in(seeds[3], 3), (K * N_RX * N_RY) // K)
    sample_owner = jax.vmap(lambda own, number: assign_block(jax.random.fold_in(seeds[3], 2), own, number, K, N_RY, 1, CAP, 2))(sample_owner_keys, sample_owner_turns).reshape((K * N_RX * N_RY, 1))
    return {"panel": panel, "signs": signs, "sample_block": sample_block, "sample_owner": sample_owner}


PRECISE = lax.Precision.HIGHEST

def hadamard(length):
    index_set = jnp.arange(length, dtype=jnp.int32)
    intersection = jnp.bitwise_and(index_set[:, None], index_set[None, :])
    parity = jnp.zeros((length, length), jnp.int32)
    for bit_index in range(max(length.bit_length() - 1, 1)):
        parity = parity + jnp.bitwise_and(jnp.right_shift(intersection, bit_index), 1)
    return (1.0 - 2.0 * jnp.bitwise_and(parity, 1)).astype(jnp.float32)

def triangle(matrix):
    col_count, row_count = matrix.shape
    index_set = jnp.arange(row_count, dtype=jnp.int32)

    def reflect(column_id, current):
        column = lax.dynamic_index_in_dim(current, column_id, 0, keepdims=False)
        below = jnp.where(index_set >= column_id, column, jnp.zeros_like(column))
        head_value = lax.dynamic_index_in_dim(column, column_id, 0, keepdims=False)
        col_norm = jnp.sqrt(jnp.sum(below * below))
        sign_value = jnp.where(head_value >= 0, 1.0, -1.0).astype(current.dtype)
        alpha_value = -sign_value * col_norm
        vector = below - alpha_value * (index_set == column_id).astype(current.dtype)
        beta_value = jnp.sum(vector * vector)
        safe_beta = jnp.where(beta_value > 0, beta_value, jnp.ones_like(beta_value))
        factor_coef = jnp.where(beta_value > 0, 2.0 / safe_beta, jnp.zeros_like(beta_value))
        projection = jnp.dot(current, vector, precision=PRECISE)
        return current - factor_coef * projection[:, None] * vector[None, :]
    reduced = lax.fori_loop(0, col_count, reflect, matrix)
    square = reduced[:, :col_count]
    col_ids = jnp.arange(col_count, dtype=jnp.int32)
    upper = jnp.where(col_ids[None, :] <= col_ids[:, None], square, jnp.zeros_like(square))
    diagonal = jnp.diagonal(upper)
    sign_flip = jnp.where(diagonal >= 0, 1.0, -1.0).astype(matrix.dtype)
    return upper * sign_flip[None, :]

def lower_inverse(lower):
    order = lower.shape[0]
    identity = jnp.eye(order, dtype=lower.dtype)

    def one_row(row_id, inverse):
        row_vals = lax.dynamic_index_in_dim(lower, row_id, 0, keepdims=False)
        unit_row = lax.dynamic_index_in_dim(identity, row_id, 0, keepdims=False)
        pivot = lax.dynamic_index_in_dim(row_vals, row_id, 0, keepdims=False)
        new_row = (unit_row - jnp.dot(row_vals, inverse, precision=PRECISE)) / pivot
        return lax.dynamic_update_index_in_dim(inverse, new_row, row_id, 0)
    return lax.fori_loop(0, order, one_row, jnp.zeros_like(lower))

def place_blocks(blocks, pick_ids, owner_ids, slot_count):
    picked = jnp.take(blocks, pick_ids, axis=1)
    order_ids = jnp.arange(owner_ids.shape[0], dtype=jnp.int32)
    earlier = jnp.logical_and(owner_ids[:, None] == owner_ids[None, :], order_ids[None, :] < order_ids[:, None])
    rank_slot = lax.optimization_barrier(jnp.sum(earlier.astype(jnp.int32), axis=1))
    slot_index = owner_ids * CAP + rank_slot
    one_hot = (jnp.arange(slot_count, dtype=jnp.int32)[:, None] == slot_index[None, :]).astype(blocks.dtype)
    return jnp.einsum('sk,ckb->csb', one_hot, picked, precision=PRECISE)

def reference(panel, signs, sample_block, sample_owner):
    device_count = N_RX * N_RY
    block_rows = R_DEV // 128
    signed = panel * signs.astype(jnp.float32)[None, :]
    blocked = signed.reshape(COLS, device_count, block_rows, 128)
    blocked = jnp.einsum('cpab,bk->cpak', blocked, hadamard(128), precision=PRECISE)
    blocked = jnp.einsum('cpab,ak->cpkb', blocked, hadamard(block_rows), precision=PRECISE)
    blocked = blocked * (1.0 / jnp.sqrt(jnp.float32(ROWS)))
    blocked = jnp.einsum('cpab,pq->cqab', blocked, hadamard(device_count), precision=PRECISE)
    mixed = blocked.reshape(COLS, ROWS)
    blocks = mixed.reshape(COLS, device_count, BLK_DEV, BLOCK)
    pick_table = sample_block.reshape(device_count, K).astype(jnp.int32)
    owner_table = sample_owner.reshape(device_count, K).astype(jnp.int32)

    def source(device):
        own_blocks = lax.dynamic_index_in_dim(blocks, device, 1, keepdims=False)
        pick_ids = lax.dynamic_index_in_dim(pick_table, device, 0, keepdims=False)
        owner_ids = lax.dynamic_index_in_dim(owner_table, device, 0, keepdims=False)
        return place_blocks(own_blocks, pick_ids, owner_ids, SLOTS)
    sent_blocks = lax.map(source, jnp.arange(device_count, dtype=jnp.int32))
    sent_blocks = sent_blocks.reshape(N_RX, N_RY, COLS, N_RY, CAP, BLOCK)
    sketch_blocks = jnp.transpose(sent_blocks, (2, 0, 3, 1, 4, 5)).reshape(COLS, device_count * SLOTS, BLOCK)

    def leaf(device):
        start = (device * SLOTS).astype(jnp.int32)
        owned = lax.dynamic_slice_in_dim(sketch_blocks, start, SLOTS, 1)
        return triangle(owned.reshape(COLS, SLOTS * BLOCK))
    leaves = lax.map(leaf, jnp.arange(device_count, dtype=jnp.int32))
    stacked = jnp.transpose(leaves, (1, 0, 2)).reshape(COLS, device_count * COLS)
    factor = triangle(stacked)
    r_factor = factor.T / jnp.sqrt(jnp.float32(SKETCH))
    inverse = lower_inverse(r_factor.T)
    solved = jnp.dot(inverse, panel, precision=PRECISE)
    leverage = lax.optimization_barrier(jnp.sum(solved * solved, axis=0)) / COLS
    return (mixed, sketch_blocks, r_factor, leverage)
```

```python
import functools
import math

import jax
import jax.numpy as jnp
from jax import lax
from jax.experimental import pallas as pl
from jax.experimental.pallas import tpu as pltpu
from jax.sharding import PartitionSpec as P

BLOCK = 128
K = 24
CAP = 4
LANES = 128
SUB = 8
STRIP = 2048

PRECISE = lax.Precision.HIGHEST


def hadamard(length):
    index_set = jnp.arange(length, dtype=jnp.int32)
    intersection = jnp.bitwise_and(index_set[:, None], index_set[None, :])
    parity = jnp.zeros((length, length), jnp.int32)
    for bit_index in range(max(length.bit_length() - 1, 1)):
        parity = parity + jnp.bitwise_and(jnp.right_shift(intersection, bit_index), 1)
    return (1.0 - 2.0 * jnp.bitwise_and(parity, 1)).astype(jnp.float32)


def own_bit(axis, bit_index):
    return lax.rem(lax.axis_index(axis) // 2**bit_index, 2)


def partner_of(axis, bit_index):
    return lax.axis_index(axis) + 2**bit_index * (1 - 2 * own_bit(axis, bit_index))


def bits_of(sizes):
    return [
        (axis, bit)
        for axis in ("ry", "rx")
        for bit in reversed(range(sizes[axis].bit_length() - 1))
    ]


def exchange_order(sizes, chunks):
    bits = bits_of(sizes)
    half_ry = (sizes["ry"].bit_length() - 1) // 2
    far = [b for b in bits if b[0] == "ry" and b[1] >= half_ry]
    near = [b for b in bits if b[0] == "ry" and b[1] < half_ry]
    cross = [b for b in bits if b[0] == "rx" and b[1] > 0]
    core = [b for b in bits if b[0] == "rx" and b[1] == 0]
    orders = []
    for chunk in range(chunks):
        if chunk % 2 == 0:
            orders.append(far + near + cross + core)
        else:
            orders.append(near + cross + core + far[::-1])

    def uses(bit):
        if bit in core:
            return {"core": 0.15}
        if bit in cross:
            return {"x": 2.0 ** (bit[1] - 1)}
        if bit in near:
            return {"y": 2.0 ** bit[1]}
        if bit[1] == half_ry:
            return {"edge": 1.0}
        return {"edge": 1.0, "mid": 2.0 ** (bit[1] - half_ry)}

    free, ready, stage, events = {}, [0.0] * chunks, [0] * chunks, []
    pending = []
    for chunk in range(chunks):
        pending.append((0.0, chunk))
    while pending:
        pending.sort()
        _, chunk = pending.pop(0)
        bit = orders[chunk][stage[chunk]]
        done = ready[chunk]
        for name, cost in uses(bit).items():
            done = max(done, max(free.get(name, 0.0), ready[chunk]) + cost)
        for name, cost in uses(bit).items():
            free[name] = max(free.get(name, 0.0), ready[chunk]) + cost
        events.append((done, chunk, stage[chunk]))
        ready[chunk] = done
        stage[chunk] += 1
        if stage[chunk] < len(orders[chunk]):
            pending.append((done, chunk))
    events.sort()
    return orders, [(chunk, step) for _, chunk, step in events]


def exchange_kernel(sizes, from_ref, used_ref, x_ref, mixed_ref, sketch_ref, land, staged,
                    keep, send_sem, recv_sem, out_sem, in_sem):
    col_count, row_count = x_ref.shape
    chunks = col_count // SUB
    low_count = sizes["ry"]
    bits = bits_of(sizes)
    me = lax.axis_index("ry")
    orders, events = exchange_order(sizes, chunks)

    barrier = pltpu.get_barrier_semaphore()
    greeted = 0
    for bit in bits:
        if bit[0] == "rx":
            pl.semaphore_signal(barrier, inc=1, device_id={"rx": partner_of(*bit)},
                                device_id_type=pl.DeviceIdType.MESH)
            greeted += 1
    for shift in range(1, low_count):
        pl.semaphore_signal(barrier, inc=1, device_id={"ry": lax.rem(me + shift, low_count)},
                            device_id_type=pl.DeviceIdType.MESH)
        greeted += 1
    pl.semaphore_wait(barrier, greeted)

    signs = {b: (1 - 2 * own_bit(*b)).astype(jnp.float32) for b in bits}
    waits = []

    def columns(chunk):
        return pl.ds(chunk * SUB, SUB)

    def source(chunk, step):
        if step == 0:
            return x_ref.at[columns(chunk)]
        return land.at[bits.index(orders[chunk][step - 1]), columns(chunk)]

    def send(chunk, step):
        bit = orders[chunk][step]
        where = bits.index(bit)
        copy = pltpu.make_async_remote_copy(
            src_ref=source(chunk, step),
            dst_ref=land.at[where, columns(chunk)],
            send_sem=send_sem.at[where, chunk],
            recv_sem=recv_sem.at[where, chunk],
            device_id={bit[0]: partner_of(*bit)},
            device_id_type=pl.DeviceIdType.MESH,
        )
        copy.start()
        waits.append(copy)
        return copy

    flight = {}
    for chunk in range(chunks):
        flight[chunk] = send(chunk, 0)
    arrivals = []
    for chunk, step in events:
        flight[chunk].wait_recv()
        bit = orders[chunk][step]
        last = step == len(bits) - 1
        own, other = source(chunk, step), land.at[bits.index(bit), columns(chunk)]
        into = mixed_ref.at[columns(chunk)] if last else other
        sign = signs[bit]

        def add(strip, carry, own=own, other=other, into=into, sign=sign, last=last):
            lanes = pl.ds(pl.multiple_of(strip * STRIP, STRIP), STRIP)
            total = other[:, lanes] + sign * own[:, lanes]
            into[:, lanes] = total
            if last:
                for at in range(STRIP // BLOCK):
                    keep[strip * (STRIP // BLOCK) + at] = total[:, at * BLOCK : (at + 1) * BLOCK]
            return carry

        lax.fori_loop(0, row_count // STRIP, add, 0)
        if not last:
            flight[chunk] = send(chunk, step + 1)
            continue

        def place(slot, carry, chunk=chunk):
            staged[slot, columns(chunk), :] = keep[from_ref[slot]] * used_ref[slot]
            return carry

        lax.fori_loop(0, low_count * CAP, place, 0)
        own_slots = pl.ds(me * CAP, CAP)
        for shift in range(1, low_count):
            to = lax.rem(me + shift, low_count)
            copy = pltpu.make_async_remote_copy(
                src_ref=staged.at[pl.ds(to * CAP, CAP), columns(chunk)],
                dst_ref=sketch_ref.at[own_slots, columns(chunk)],
                send_sem=out_sem.at[shift - 1, chunk],
                recv_sem=in_sem.at[shift - 1, chunk],
                device_id={"ry": to},
                device_id_type=pl.DeviceIdType.MESH,
            )
            copy.start()
            arrivals.append(copy)
        sketch_ref[own_slots, columns(chunk), :] = staged[own_slots, columns(chunk), :]
    for copy in arrivals:
        copy.wait()
    for copy in waits:
        copy.wait_send()


def exchange(sizes, x, from_block, used):
    col_count, row_count = x.shape
    chunks = col_count // SUB
    slots = sizes["ry"] * CAP
    bit_count = len(bits_of(sizes))
    vmem = pl.BlockSpec(memory_space=pltpu.VMEM)
    smem = pl.BlockSpec(memory_space=pltpu.SMEM)
    return pl.pallas_call(
        functools.partial(exchange_kernel, sizes),
        out_shape=(
            jax.ShapeDtypeStruct((col_count, row_count), jnp.float32),
            jax.ShapeDtypeStruct((slots, col_count, BLOCK), jnp.float32),
        ),
        in_specs=[smem, smem, vmem],
        out_specs=(vmem, vmem),
        scratch_shapes=[
            pltpu.VMEM((bit_count, col_count, row_count), jnp.float32),
            pltpu.VMEM((slots, col_count, BLOCK), jnp.float32),
            pltpu.VMEM((row_count // BLOCK, SUB, BLOCK), jnp.float32),
            pltpu.SemaphoreType.DMA((bit_count, chunks)),
            pltpu.SemaphoreType.DMA((bit_count, chunks)),
            pltpu.SemaphoreType.DMA((sizes["ry"] - 1, chunks)),
            pltpu.SemaphoreType.DMA((sizes["ry"] - 1, chunks)),
        ],
        compiler_params=pltpu.CompilerParams(
            collective_id=0, has_side_effects=True, vmem_limit_bytes=50 * 2**20
        ),
        name="exchange",
    )(from_block, used, x)


def reduce_columns(work):
    tiles, col_count, _ = work.shape
    lane = lax.broadcasted_iota(jnp.int32, (1, LANES), 1)
    for low in range(0, col_count, SUB):
        rest = slice(low, col_count)

        def reflect(column, carry, low=low, rest=rest):
            at = pl.ds(column, 1)
            here = lane == column
            below = jnp.where(lane >= column, work[0, at, :], 0.0)
            top = work[0, rest, :]
            square = below * below
            product = top * below
            for tile in range(1, tiles):
                vector = work[tile, at, :]
                square = square + vector * vector
                product = product + work[tile, rest, :] * vector
            norm2 = jnp.sum(square, axis=1, keepdims=True)
            head = jnp.sum(jnp.where(here, below, 0.0), axis=1, keepdims=True)
            across = jnp.sum(jnp.where(here, top, 0.0), axis=1, keepdims=True)
            product = jnp.sum(product, axis=1, keepdims=True)
            norm = jnp.sqrt(norm2)
            alpha = jnp.where(head >= 0, -norm, norm)
            half = norm2 + jnp.abs(head) * norm
            coef = jnp.where(half > 0, 1.0 / jnp.where(half > 0, half, 1.0), 0.0)
            project = coef * (product - alpha * across)
            first = below - jnp.where(here, alpha, 0.0)
            vectors = [first] + [work[tile, at, :] for tile in range(1, tiles)]
            for tile in range(tiles):
                work[tile, rest, :] = work[tile, rest, :] - project * vectors[tile]
            return carry

        lax.fori_loop(low, low + SUB, reflect, 0)
    square = work[0]
    row_id = lax.broadcasted_iota(jnp.int32, (col_count, LANES), 0)
    lane_id = lax.broadcasted_iota(jnp.int32, (col_count, LANES), 1)
    upper = jnp.where(lane_id <= row_id, square, 0.0)
    diagonal = jnp.sum(jnp.where(lane_id == row_id, upper, 0.0), axis=0, keepdims=True)
    return upper * jnp.where(diagonal >= 0, 1.0, -1.0)


def leaf_kernel(sketch_ref, leaf_ref, work):
    work[...] = sketch_ref[...]
    factor = reduce_columns(work)
    half = factor.shape[0] // 2
    lane = lax.broadcasted_iota(jnp.int32, (half, LANES), 1)
    leaf_ref[...] = jnp.where(lane < LANES // 2, factor[:half], pltpu.roll(factor[half:], LANES // 2, 1))


def leaf(sketch):
    _, col_count, _ = sketch.shape
    return pl.pallas_call(
        leaf_kernel,
        out_shape=jax.ShapeDtypeStruct((col_count // 2, LANES), jnp.float32),
        in_specs=[pl.BlockSpec(memory_space=pltpu.VMEM)],
        out_specs=pl.BlockSpec(memory_space=pltpu.VMEM),
        scratch_shapes=[pltpu.VMEM(sketch.shape, jnp.float32)],
        compiler_params=pltpu.CompilerParams(vmem_limit_bytes=16 * 2**20),
        name="leaf",
    )(sketch)


def gather_kernel(sizes, leaf_ref, all_ref, send_sem, recv_sem):
    bits = bits_of(sizes)
    barrier = pltpu.get_barrier_semaphore()
    for bit in bits:
        pl.semaphore_signal(barrier, inc=1, device_id={bit[0]: partner_of(*bit)},
                            device_id_type=pl.DeviceIdType.MESH)
    pl.semaphore_wait(barrier, len(bits))
    place = 0
    for level, bit in enumerate(bits):
        place = place + 2**level * own_bit(*bit)
    all_ref[pl.ds(place, 1)] = leaf_ref[...][None]
    for level, bit in enumerate(bits):
        width = 2**level
        held = all_ref.at[pl.ds(place // width * width, width)]
        copy = pltpu.make_async_remote_copy(
            src_ref=held, dst_ref=held,
            send_sem=send_sem.at[level], recv_sem=recv_sem.at[level],
            device_id={bit[0]: partner_of(*bit)}, device_id_type=pl.DeviceIdType.MESH,
        )
        copy.start()
        copy.wait()


def gather(sizes, leaf_factor):
    bit_count = len(bits_of(sizes))
    return pl.pallas_call(
        functools.partial(gather_kernel, sizes),
        out_shape=jax.ShapeDtypeStruct((sizes["rx"] * sizes["ry"],) + leaf_factor.shape, jnp.float32),
        in_specs=[pl.BlockSpec(memory_space=pltpu.VMEM)],
        out_specs=pl.BlockSpec(memory_space=pltpu.VMEM),
        scratch_shapes=[pltpu.SemaphoreType.DMA((bit_count,)), pltpu.SemaphoreType.DMA((bit_count,))],
        compiler_params=pltpu.CompilerParams(collective_id=1, has_side_effects=True),
        name="gather",
    )(leaf_factor)


def final_kernel(scale, all_ref, lower_ref, inverse_ref, work):
    leaves, half, _ = all_ref.shape
    col_count = 2 * half
    lane = lax.broadcasted_iota(jnp.int32, (half, LANES), 1)
    left = lane < LANES // 2
    for tile in range(leaves // 2):
        one, two = all_ref[2 * tile], all_ref[2 * tile + 1]
        work[tile, :half, :] = jnp.where(left, one, pltpu.roll(two, LANES // 2, 1))
        work[tile, half:, :] = jnp.where(left, pltpu.roll(one, LANES // 2, 1), two)
    lower = reduce_columns(work) / scale
    lower_ref[...] = lower
    row_id = lax.broadcasted_iota(jnp.int32, (SUB, LANES), 0)
    lane_id = lax.broadcasted_iota(jnp.int32, (SUB, LANES), 1)
    parts = [
        jnp.where(lane_id == row_id + SUB * part, 1.0, 0.0) for part in range(col_count // SUB)
    ]
    for row in range(col_count):
        part, at = divmod(row, SUB)
        solved = parts[part][at : at + 1, :] / lower[row : row + 1, row : row + 1]
        for later in range(part, col_count // SUB):
            factor = lower[later * SUB : (later + 1) * SUB, row : row + 1]
            reduced = parts[later] - factor * solved
            if later == part:
                reduced = jnp.where(
                    row_id == at, solved, jnp.where(row_id > at, reduced, parts[later])
                )
            parts[later] = reduced
    for part in range(col_count // SUB):
        inverse_ref[part * SUB : (part + 1) * SUB, :] = parts[part]


def final(all_leaves, scale):
    leaves, half, _ = all_leaves.shape
    col_count = 2 * half
    shape = jax.ShapeDtypeStruct((col_count, LANES), jnp.float32)
    vmem = pl.BlockSpec(memory_space=pltpu.VMEM)
    return pl.pallas_call(
        functools.partial(final_kernel, scale),
        out_shape=(shape, shape),
        in_specs=[vmem],
        out_specs=(vmem, vmem),
        scratch_shapes=[pltpu.VMEM((leaves // 2, col_count, LANES), jnp.float32)],
        compiler_params=pltpu.CompilerParams(vmem_limit_bytes=16 * 2**20),
        name="final",
    )(all_leaves)


def slot_sources(pick_ids, owner_ids, slot_count):
    order_ids = jnp.arange(owner_ids.shape[0], dtype=jnp.int32)
    earlier = jnp.logical_and(
        owner_ids[:, None] == owner_ids[None, :], order_ids[None, :] < order_ids[:, None]
    )
    rank_slot = jnp.sum(earlier.astype(jnp.int32), axis=1)
    slot_index = owner_ids * CAP + rank_slot
    match = (jnp.arange(slot_count, dtype=jnp.int32)[:, None] == slot_index[None, :]).astype(jnp.int32)
    return jnp.sum(match * pick_ids[None, :], axis=1), jnp.sum(match, axis=1).astype(jnp.float32)


def per_device(sizes, panel, signs, sample_block, sample_owner):
    col_count, row_count = panel.shape
    block_rows = row_count // LANES
    device_count = sizes["ry"] * sizes["rx"]
    from_block, used = slot_sources(sample_block, sample_owner[:, 0], sizes["ry"] * CAP)
    signed = panel * signs.astype(jnp.float32)[None, :]
    blocked = signed.reshape(col_count, block_rows, LANES)
    blocked = jnp.einsum("cab,bk->cak", blocked, hadamard(LANES), precision=PRECISE)
    blocked = jnp.einsum("cab,ak->ckb", blocked, hadamard(block_rows), precision=PRECISE)
    local = blocked.reshape(col_count, row_count) * (1.0 / math.sqrt(row_count * device_count))
    mixed, sketch = exchange(sizes, local, from_block, used)
    received = jnp.transpose(sketch, (1, 0, 2))
    all_leaves = gather(sizes, leaf(sketch))
    lower, inverse = final(all_leaves, math.sqrt(K * BLOCK * device_count))
    r_factor = lower[:, :col_count].T
    solved = jnp.dot(inverse[:, :col_count], panel, precision=PRECISE)
    leverage = jnp.sum(solved * solved, axis=0) / col_count
    return (mixed, received, r_factor, leverage)


def solution(mesh):
    sizes = {name: int(mesh.shape[name]) for name in ("rx", "ry")}
    in_specs = (P(None, ("rx", "ry")), P(("rx", "ry")), P(("rx", "ry")), P(("rx", "ry"), None))
    out_specs = (P(None, ("rx", "ry")), P(None, ("rx", "ry"), None), P(), P(("rx", "ry")))
    return jax.shard_map(
        functools.partial(per_device, sizes), mesh=mesh, in_specs=in_specs, out_specs=out_specs,
        check_vma=False,
    )
```

```python
import functools
import math

import jax
import jax.numpy as jnp
from jax import lax
from jax.experimental import pallas as pl
from jax.experimental.pallas import tpu as pltpu
from jax.sharding import PartitionSpec as P

BLOCK = 128
K = 24
CAP = 4
LANES = 128
SUB = 8
STRIP = 2048
PARTS = 2
DEPTH = 2

PRECISE = lax.Precision.HIGHEST


def hadamard(length):
    index_set = jnp.arange(length, dtype=jnp.int32)
    intersection = jnp.bitwise_and(index_set[:, None], index_set[None, :])
    parity = jnp.zeros((length, length), jnp.int32)
    for bit_index in range(max(length.bit_length() - 1, 1)):
        parity = parity + jnp.bitwise_and(jnp.right_shift(intersection, bit_index), 1)
    return (1.0 - 2.0 * jnp.bitwise_and(parity, 1)).astype(jnp.float32)


def own_bit(axis, bit_index):
    return lax.rem(lax.axis_index(axis) // 2**bit_index, 2)


def partner_of(axis, bit_index):
    return lax.axis_index(axis) + 2**bit_index * (1 - 2 * own_bit(axis, bit_index))


def bits_of(sizes):
    return [
        (axis, bit)
        for axis in ("ry", "rx")
        for bit in reversed(range(sizes[axis].bit_length() - 1))
    ]


def exchange_plan(sizes, units):
    bits = bits_of(sizes)
    half_ry = (sizes["ry"].bit_length() - 1) // 2
    far = [b for b in bits if b[0] == "ry" and b[1] >= half_ry]
    near = [b for b in bits if b[0] == "ry" and b[1] < half_ry]
    cross = [b for b in bits if b[0] == "rx" and b[1] > 0]
    core = [b for b in bits if b[0] == "rx" and b[1] == 0]
    orders = []
    for unit in range(units):
        deep = far if unit % 2 == 0 else far[::-1]
        rest = near + cross + core if unit // 2 % 2 == 0 else cross + core + near
        orders.append(deep + rest if unit < units // 2 else rest + deep)

    def uses(bit):
        if bit in core:
            return {"core": 0.15}
        if bit in cross:
            return {"x": 2.0 ** (bit[1] - 1)}
        if bit in near:
            return {"y": 2.0 ** bit[1]}
        if bit[1] == half_ry:
            return {"edge": 1.0}
        return {"edge": 1.0, "mid": 2.0 ** (bit[1] - half_ry)}

    active, steps = {}, []
    waiting = {bit: [(unit, 0) for unit in range(units) if orders[unit][0] == bit] for bit in bits}
    counts = {bit: 0 for bit in bits}

    def admit(bit):
        waiting[bit].sort()
        while waiting[bit] and counts[bit] < DEPTH:
            unit, step = waiting[bit].pop(0)
            counts[bit] += 1
            active[(unit, step)] = 1.0
            steps.append(("start", unit, step))

    for bit in bits:
        admit(bit)
    while active:
        load = {}
        for unit, step in active:
            for name, cost in uses(orders[unit][step]).items():
                load[name] = load.get(name, 0.0) + cost
        rates = {
            key: 1.0 / max(load[name] for name in uses(orders[key[0]][key[1]])) for key in active
        }
        span, unit, step = min((active[key] / rates[key],) + key for key in active)
        for key in active:
            active[key] -= span * rates[key]
        del active[(unit, step)]
        bit = orders[unit][step]
        counts[bit] -= 1
        steps.append(("take", unit, step))
        admit(bit)
        steps.append(("add", unit, step))
        if step + 1 < len(bits):
            waiting[orders[unit][step + 1]].append((unit, step + 1))
            admit(orders[unit][step + 1])
    return orders, steps


def exchange_kernel(sizes, from_ref, used_ref, x_ref, mixed_ref, sketch_ref, land, staged,
                    keep, send_sem, recv_sem, out_sem, in_sem):
    col_count, row_count = x_ref.shape
    chunks = col_count // SUB
    low_count = sizes["ry"]
    bits = bits_of(sizes)
    me = lax.axis_index("ry")
    units = chunks * PARTS
    part = row_count // PARTS
    orders, steps = exchange_plan(sizes, units)

    barrier = pltpu.get_barrier_semaphore()
    greeted = 0
    for bit in bits:
        if bit[0] == "rx":
            pl.semaphore_signal(barrier, inc=1, device_id={"rx": partner_of(*bit)},
                                device_id_type=pl.DeviceIdType.MESH)
            greeted += 1
    for shift in range(1, low_count):
        pl.semaphore_signal(barrier, inc=1, device_id={"ry": lax.rem(me + shift, low_count)},
                            device_id_type=pl.DeviceIdType.MESH)
        greeted += 1
    pl.semaphore_wait(barrier, greeted)

    signs = {b: (1 - 2 * own_bit(*b)).astype(jnp.float32) for b in bits}
    waits = []

    def columns(chunk):
        return pl.ds(chunk * SUB, SUB)

    def piece(unit):
        return columns(unit // PARTS), pl.ds(unit % PARTS * part, part)

    def source(unit, step):
        if step == 0:
            return x_ref.at[piece(unit)]
        return land.at[(bits.index(orders[unit][step - 1]),) + piece(unit)]

    flight, arrivals, done = {}, [], [0] * chunks
    for kind, unit, step in steps:
        bit = orders[unit][step]
        where = bits.index(bit)
        own, other = source(unit, step), land.at[(where,) + piece(unit)]
        if kind == "start":
            copy = pltpu.make_async_remote_copy(
                src_ref=own,
                dst_ref=other,
                send_sem=send_sem.at[where, unit],
                recv_sem=recv_sem.at[where, unit],
                device_id={bit[0]: partner_of(*bit)},
                device_id_type=pl.DeviceIdType.MESH,
            )
            copy.start()
            waits.append(copy)
            flight[unit] = copy
            continue
        if kind == "take":
            flight[unit].wait_recv()
            continue
        chunk = unit // PARTS
        last = step == len(bits) - 1
        into = mixed_ref.at[piece(unit)] if last else other
        first = unit % PARTS * part // BLOCK
        sign = signs[bit]

        def add(strip, carry, own=own, other=other, into=into, sign=sign, last=last, first=first):
            lanes = pl.ds(pl.multiple_of(strip * STRIP, STRIP), STRIP)
            total = other[:, lanes] + sign * own[:, lanes]
            into[:, lanes] = total
            if last:
                for at in range(STRIP // BLOCK):
                    block = total[:, at * BLOCK : (at + 1) * BLOCK]
                    keep[chunk_slot, first + strip * (STRIP // BLOCK) + at] = block
            return carry

        chunk_slot = chunk
        lax.fori_loop(0, part // STRIP, add, 0)
        if not last:
            continue
        done[chunk] += 1
        if done[chunk] < PARTS:
            continue

        def place(slot, carry, chunk=chunk):
            staged[slot, columns(chunk), :] = keep[chunk, from_ref[slot]] * used_ref[slot]
            return carry

        lax.fori_loop(0, low_count * CAP, place, 0)
        own_slots = pl.ds(me * CAP, CAP)
        for shift in range(1, low_count):
            to = lax.rem(me + shift, low_count)
            copy = pltpu.make_async_remote_copy(
                src_ref=staged.at[pl.ds(to * CAP, CAP), columns(chunk)],
                dst_ref=sketch_ref.at[own_slots, columns(chunk)],
                send_sem=out_sem.at[shift - 1, chunk],
                recv_sem=in_sem.at[shift - 1, chunk],
                device_id={"ry": to},
                device_id_type=pl.DeviceIdType.MESH,
            )
            copy.start()
            arrivals.append(copy)
        sketch_ref[own_slots, columns(chunk), :] = staged[own_slots, columns(chunk), :]
    for copy in arrivals:
        copy.wait()
    for copy in waits:
        copy.wait_send()


def exchange(sizes, x, from_block, used):
    col_count, row_count = x.shape
    chunks = col_count // SUB
    slots = sizes["ry"] * CAP
    bit_count = len(bits_of(sizes))
    vmem = pl.BlockSpec(memory_space=pltpu.VMEM)
    smem = pl.BlockSpec(memory_space=pltpu.SMEM)
    return pl.pallas_call(
        functools.partial(exchange_kernel, sizes),
        out_shape=(
            jax.ShapeDtypeStruct((col_count, row_count), jnp.float32),
            jax.ShapeDtypeStruct((slots, col_count, BLOCK), jnp.float32),
        ),
        in_specs=[smem, smem, vmem],
        out_specs=(vmem, vmem),
        scratch_shapes=[
            pltpu.VMEM((bit_count, col_count, row_count), jnp.float32),
            pltpu.VMEM((slots, col_count, BLOCK), jnp.float32),
            pltpu.VMEM((chunks, row_count // BLOCK, SUB, BLOCK), jnp.float32),
            pltpu.SemaphoreType.DMA((bit_count, chunks * PARTS)),
            pltpu.SemaphoreType.DMA((bit_count, chunks * PARTS)),
            pltpu.SemaphoreType.DMA((sizes["ry"] - 1, chunks)),
            pltpu.SemaphoreType.DMA((sizes["ry"] - 1, chunks)),
        ],
        compiler_params=pltpu.CompilerParams(
            collective_id=0, has_side_effects=True, vmem_limit_bytes=50 * 2**20
        ),
        name="exchange",
    )(from_block, used, x)


def reduce_columns(work):
    tiles, col_count, _ = work.shape
    lane = lax.broadcasted_iota(jnp.int32, (1, LANES), 1)
    for low in range(0, col_count, SUB):
        rest = slice(low, col_count)

        def reflect(column, carry, low=low, rest=rest):
            at = pl.ds(column, 1)
            here = lane == column
            below = jnp.where(lane >= column, work[0, at, :], 0.0)
            top = work[0, rest, :]
            square = below * below
            product = top * below
            for tile in range(1, tiles):
                vector = work[tile, at, :]
                square = square + vector * vector
                product = product + work[tile, rest, :] * vector
            norm2 = jnp.sum(square, axis=1, keepdims=True)
            head = jnp.sum(jnp.where(here, below, 0.0), axis=1, keepdims=True)
            across = jnp.sum(jnp.where(here, top, 0.0), axis=1, keepdims=True)
            product = jnp.sum(product, axis=1, keepdims=True)
            norm = jnp.sqrt(norm2)
            alpha = jnp.where(head >= 0, -norm, norm)
            half = norm2 + jnp.abs(head) * norm
            coef = jnp.where(half > 0, 1.0 / jnp.where(half > 0, half, 1.0), 0.0)
            project = coef * (product - alpha * across)
            first = below - jnp.where(here, alpha, 0.0)
            vectors = [first] + [work[tile, at, :] for tile in range(1, tiles)]
            for tile in range(tiles):
                work[tile, rest, :] = work[tile, rest, :] - project * vectors[tile]
            return carry

        lax.fori_loop(low, low + SUB, reflect, 0)
    square = work[0]
    row_id = lax.broadcasted_iota(jnp.int32, (col_count, LANES), 0)
    lane_id = lax.broadcasted_iota(jnp.int32, (col_count, LANES), 1)
    upper = jnp.where(lane_id <= row_id, square, 0.0)
    diagonal = jnp.sum(jnp.where(lane_id == row_id, upper, 0.0), axis=0, keepdims=True)
    return upper * jnp.where(diagonal >= 0, 1.0, -1.0)


def leaf_kernel(sketch_ref, leaf_ref, work):
    work[...] = sketch_ref[...]
    factor = reduce_columns(work)
    half = factor.shape[0] // 2
    lane = lax.broadcasted_iota(jnp.int32, (half, LANES), 1)
    leaf_ref[...] = jnp.where(lane < LANES // 2, factor[:half], pltpu.roll(factor[half:], LANES // 2, 1))


def leaf(sketch):
    _, col_count, _ = sketch.shape
    return pl.pallas_call(
        leaf_kernel,
        out_shape=jax.ShapeDtypeStruct((col_count // 2, LANES), jnp.float32),
        in_specs=[pl.BlockSpec(memory_space=pltpu.VMEM)],
        out_specs=pl.BlockSpec(memory_space=pltpu.VMEM),
        scratch_shapes=[pltpu.VMEM(sketch.shape, jnp.float32)],
        compiler_params=pltpu.CompilerParams(vmem_limit_bytes=16 * 2**20),
        name="leaf",
    )(sketch)


def gather_kernel(sizes, leaf_ref, all_ref, send_sem, recv_sem, near_send, near_recv):
    low_count = sizes["ry"]
    bits = [bit for bit in bits_of(sizes) if bit[0] == "rx"]
    me = lax.axis_index("ry")
    barrier = pltpu.get_barrier_semaphore()
    for bit in bits:
        pl.semaphore_signal(barrier, inc=1, device_id={"rx": partner_of(*bit)},
                            device_id_type=pl.DeviceIdType.MESH)
    for shift in range(1, low_count):
        pl.semaphore_signal(barrier, inc=1, device_id={"ry": lax.rem(me + shift, low_count)},
                            device_id_type=pl.DeviceIdType.MESH)
    pl.semaphore_wait(barrier, len(bits) + low_count - 1)
    group = 0
    for level, bit in enumerate(bits):
        group = group + 2**level * own_bit(*bit)
    place = pl.ds(group * low_count + me, 1)
    all_ref[place] = leaf_ref[...][None]
    copies = []
    for shift in range(1, low_count):
        copy = pltpu.make_async_remote_copy(
            src_ref=all_ref.at[place], dst_ref=all_ref.at[place],
            send_sem=near_send.at[shift - 1], recv_sem=near_recv.at[shift - 1],
            device_id={"ry": lax.rem(me + shift, low_count)},
            device_id_type=pl.DeviceIdType.MESH,
        )
        copy.start()
        copies.append(copy)
    for copy in copies:
        copy.wait()
    for level, bit in enumerate(bits):
        width = 2**level
        held = all_ref.at[pl.ds(group // width * width * low_count, width * low_count)]
        copy = pltpu.make_async_remote_copy(
            src_ref=held, dst_ref=held,
            send_sem=send_sem.at[level], recv_sem=recv_sem.at[level],
            device_id={"rx": partner_of(*bit)}, device_id_type=pl.DeviceIdType.MESH,
        )
        copy.start()
        copy.wait()


def gather(sizes, leaf_factor):
    bit_count = len(bits_of(sizes))
    return pl.pallas_call(
        functools.partial(gather_kernel, sizes),
        out_shape=jax.ShapeDtypeStruct((sizes["rx"] * sizes["ry"],) + leaf_factor.shape, jnp.float32),
        in_specs=[pl.BlockSpec(memory_space=pltpu.VMEM)],
        out_specs=pl.BlockSpec(memory_space=pltpu.VMEM),
        scratch_shapes=[
            pltpu.SemaphoreType.DMA((bit_count,)),
            pltpu.SemaphoreType.DMA((bit_count,)),
            pltpu.SemaphoreType.DMA((sizes["ry"] - 1,)),
            pltpu.SemaphoreType.DMA((sizes["ry"] - 1,)),
        ],
        compiler_params=pltpu.CompilerParams(collective_id=1, has_side_effects=True),
        name="gather",
    )(leaf_factor)


def final_kernel(scale, all_ref, lower_ref, inverse_ref, work):
    leaves, half, _ = all_ref.shape
    col_count = 2 * half
    lane = lax.broadcasted_iota(jnp.int32, (half, LANES), 1)
    left = lane < LANES // 2
    for tile in range(leaves // 2):
        one, two = all_ref[2 * tile], all_ref[2 * tile + 1]
        work[tile, :half, :] = jnp.where(left, one, pltpu.roll(two, LANES // 2, 1))
        work[tile, half:, :] = jnp.where(left, pltpu.roll(one, LANES // 2, 1), two)
    lower = reduce_columns(work) / scale
    lower_ref[...] = lower
    row_id = lax.broadcasted_iota(jnp.int32, (SUB, LANES), 0)
    lane_id = lax.broadcasted_iota(jnp.int32, (SUB, LANES), 1)
    parts = [
        jnp.where(lane_id == row_id + SUB * part, 1.0, 0.0) for part in range(col_count // SUB)
    ]
    for row in range(col_count):
        part, at = divmod(row, SUB)
        solved = parts[part][at : at + 1, :] / lower[row : row + 1, row : row + 1]
        for later in range(part, col_count // SUB):
            factor = lower[later * SUB : (later + 1) * SUB, row : row + 1]
            reduced = parts[later] - factor * solved
            if later == part:
                reduced = jnp.where(
                    row_id == at, solved, jnp.where(row_id > at, reduced, parts[later])
                )
            parts[later] = reduced
    for part in range(col_count // SUB):
        inverse_ref[part * SUB : (part + 1) * SUB, :] = parts[part]


def final(all_leaves, scale):
    leaves, half, _ = all_leaves.shape
    col_count = 2 * half
    shape = jax.ShapeDtypeStruct((col_count, LANES), jnp.float32)
    vmem = pl.BlockSpec(memory_space=pltpu.VMEM)
    return pl.pallas_call(
        functools.partial(final_kernel, scale),
        out_shape=(shape, shape),
        in_specs=[vmem],
        out_specs=(vmem, vmem),
        scratch_shapes=[pltpu.VMEM((leaves // 2, col_count, LANES), jnp.float32)],
        compiler_params=pltpu.CompilerParams(vmem_limit_bytes=16 * 2**20),
        name="final",
    )(all_leaves)


def slot_sources(pick_ids, owner_ids, slot_count):
    order_ids = jnp.arange(owner_ids.shape[0], dtype=jnp.int32)
    earlier = jnp.logical_and(
        owner_ids[:, None] == owner_ids[None, :], order_ids[None, :] < order_ids[:, None]
    )
    rank_slot = jnp.sum(earlier.astype(jnp.int32), axis=1)
    slot_index = owner_ids * CAP + rank_slot
    match = (jnp.arange(slot_count, dtype=jnp.int32)[:, None] == slot_index[None, :]).astype(jnp.int32)
    return jnp.sum(match * pick_ids[None, :], axis=1), jnp.sum(match, axis=1).astype(jnp.float32)


def per_device(sizes, panel, signs, sample_block, sample_owner):
    col_count, row_count = panel.shape
    block_rows = row_count // LANES
    device_count = sizes["ry"] * sizes["rx"]
    from_block, used = slot_sources(sample_block, sample_owner[:, 0], sizes["ry"] * CAP)
    signed = panel * signs.astype(jnp.float32)[None, :]
    blocked = signed.reshape(col_count, block_rows, LANES)
    blocked = jnp.einsum("cab,bk->cak", blocked, hadamard(LANES), precision=PRECISE)
    blocked = jnp.einsum("cab,ak->ckb", blocked, hadamard(block_rows), precision=PRECISE)
    local = blocked.reshape(col_count, row_count) * (1.0 / math.sqrt(row_count * device_count))
    mixed, sketch = exchange(sizes, local, from_block, used)
    received = jnp.transpose(sketch, (1, 0, 2))
    all_leaves = gather(sizes, leaf(sketch))
    lower, inverse = final(all_leaves, math.sqrt(K * BLOCK * device_count))
    r_factor = lower[:, :col_count].T
    solved = jnp.dot(inverse[:, :col_count], panel, precision=PRECISE)
    leverage = jnp.sum(solved * solved, axis=0) / col_count
    return (mixed, received, r_factor, leverage)


def solution(mesh):
    sizes = {name: int(mesh.shape[name]) for name in ("rx", "ry")}
    in_specs = (P(None, ("rx", "ry")), P(("rx", "ry")), P(("rx", "ry")), P(("rx", "ry"), None))
    out_specs = (P(None, ("rx", "ry")), P(None, ("rx", "ry"), None), P(), P(("rx", "ry")))
    return jax.shard_map(
        functools.partial(per_device, sizes), mesh=mesh, in_specs=in_specs, out_specs=out_specs,
        check_vma=False,
    )
```

```python
import functools
import math

import jax
import jax.numpy as jnp
from jax import lax
from jax.experimental import pallas as pl
from jax.experimental.pallas import tpu as pltpu
from jax.sharding import PartitionSpec as P

BLOCK = 128
K = 24
CAP = 4
LANES = 128
SUB = 8
STRIP = 2048
PARTS = 2
DEPTH = 2

PRECISE = lax.Precision.HIGHEST


def hadamard(length):
    index_set = jnp.arange(length, dtype=jnp.int32)
    intersection = jnp.bitwise_and(index_set[:, None], index_set[None, :])
    parity = jnp.zeros((length, length), jnp.int32)
    for bit_index in range(max(length.bit_length() - 1, 1)):
        parity = parity + jnp.bitwise_and(jnp.right_shift(intersection, bit_index), 1)
    return (1.0 - 2.0 * jnp.bitwise_and(parity, 1)).astype(jnp.float32)


def own_bit(axis, bit_index):
    return lax.rem(lax.axis_index(axis) // 2**bit_index, 2)


def partner_of(axis, bit_index):
    return lax.axis_index(axis) + 2**bit_index * (1 - 2 * own_bit(axis, bit_index))


def bits_of(sizes):
    return [
        (axis, bit)
        for axis in ("ry", "rx")
        for bit in reversed(range(sizes[axis].bit_length() - 1))
    ]


def exchange_plan(sizes, units):
    bits = bits_of(sizes)
    half_ry = (sizes["ry"].bit_length() - 1) // 2
    far = [b for b in bits if b[0] == "ry" and b[1] >= half_ry]
    near = [b for b in bits if b[0] == "ry" and b[1] < half_ry]
    cross = [b for b in bits if b[0] == "rx" and b[1] > 0]
    core = [b for b in bits if b[0] == "rx" and b[1] == 0]
    orders = []
    for unit in range(units):
        deep = far if unit % 2 == 0 else far[::-1]
        rest = near + cross + core if unit // 2 % 2 == 0 else cross + core + near
        orders.append(deep + rest if unit < units // 2 else rest + deep)

    def uses(bit):
        if bit in core:
            return {"core": 0.15}
        if bit in cross:
            return {"x": 2.0 ** (bit[1] - 1)}
        if bit in near:
            return {"y": 2.0 ** bit[1]}
        if bit[1] == half_ry:
            return {"edge": 1.0}
        return {"edge": 1.0, "mid": 2.0 ** (bit[1] - half_ry)}

    active, steps = {}, []
    waiting = {bit: [(unit, 0) for unit in range(units) if orders[unit][0] == bit] for bit in bits}
    counts = {bit: 0 for bit in bits}

    def admit(bit):
        waiting[bit].sort()
        while waiting[bit] and counts[bit] < DEPTH:
            unit, step = waiting[bit].pop(0)
            counts[bit] += 1
            active[(unit, step)] = 1.0
            steps.append(("start", unit, step))

    for bit in bits:
        admit(bit)
    while active:
        load = {}
        for unit, step in active:
            for name, cost in uses(orders[unit][step]).items():
                load[name] = load.get(name, 0.0) + cost
        rates = {
            key: 1.0 / max(load[name] for name in uses(orders[key[0]][key[1]])) for key in active
        }
        span, unit, step = min((active[key] / rates[key],) + key for key in active)
        for key in active:
            active[key] -= span * rates[key]
        del active[(unit, step)]
        bit = orders[unit][step]
        counts[bit] -= 1
        steps.append(("take", unit, step))
        admit(bit)
        steps.append(("add", unit, step))
        if step + 1 < len(bits):
            waiting[orders[unit][step + 1]].append((unit, step + 1))
            admit(orders[unit][step + 1])
    return orders, steps


def exchange_kernel(sizes, from_ref, used_ref, x_ref, mixed_ref, sketch_ref, land, staged,
                    keep, local, send_sem, recv_sem, out_sem, in_sem):
    block_count, col_count, _ = x_ref.shape
    row_count = block_count * BLOCK
    chunks = col_count // SUB
    low_count = sizes["ry"]
    bits = bits_of(sizes)
    me = lax.axis_index("ry")
    units = chunks * PARTS
    part = row_count // PARTS
    orders, steps = exchange_plan(sizes, units)

    barrier = pltpu.get_barrier_semaphore()
    greeted = 0
    for bit in bits:
        if bit[0] == "rx":
            pl.semaphore_signal(barrier, inc=1, device_id={"rx": partner_of(*bit)},
                                device_id_type=pl.DeviceIdType.MESH)
            greeted += 1
    for shift in range(1, low_count):
        pl.semaphore_signal(barrier, inc=1, device_id={"ry": lax.rem(me + shift, low_count)},
                            device_id_type=pl.DeviceIdType.MESH)
        greeted += 1
    pl.semaphore_wait(barrier, greeted)

    signs = {b: (1 - 2 * own_bit(*b)).astype(jnp.float32) for b in bits}
    waits = []

    def columns(chunk):
        return pl.ds(chunk * SUB, SUB)

    def piece(unit):
        return columns(unit // PARTS), pl.ds(unit % PARTS * part, part)

    def source(unit, step):
        if step == 0:
            return local.at[piece(unit)]
        return land.at[(bits.index(orders[unit][step - 1]),) + piece(unit)]

    flight, arrivals, done = {}, [], [0] * chunks
    for kind, unit, step in steps:
        bit = orders[unit][step]
        where = bits.index(bit)
        own, other = source(unit, step), land.at[(where,) + piece(unit)]
        if kind == "start" and step == 0:
            start = unit % PARTS * part // BLOCK

            def lay(group, carry, unit=unit, start=start):
                for at in range(STRIP // BLOCK):
                    block = start + group * (STRIP // BLOCK) + at
                    lanes = pl.ds(pl.multiple_of(block * BLOCK, BLOCK), BLOCK)
                    local[columns(unit // PARTS), lanes] = x_ref[block, columns(unit // PARTS), :]
                return carry

            lax.fori_loop(0, part // STRIP, lay, 0)
        if kind == "start":
            copy = pltpu.make_async_remote_copy(
                src_ref=own,
                dst_ref=other,
                send_sem=send_sem.at[where, unit],
                recv_sem=recv_sem.at[where, unit],
                device_id={bit[0]: partner_of(*bit)},
                device_id_type=pl.DeviceIdType.MESH,
            )
            copy.start()
            waits.append(copy)
            flight[unit] = copy
            continue
        if kind == "take":
            flight[unit].wait_recv()
            continue
        chunk = unit // PARTS
        last = step == len(bits) - 1
        into = mixed_ref.at[piece(unit)] if last else other
        first = unit % PARTS * part // BLOCK
        sign = signs[bit]

        def add(strip, carry, own=own, other=other, into=into, sign=sign, last=last, first=first):
            lanes = pl.ds(pl.multiple_of(strip * STRIP, STRIP), STRIP)
            total = other[:, lanes] + sign * own[:, lanes]
            into[:, lanes] = total
            if last:
                for at in range(STRIP // BLOCK):
                    block = total[:, at * BLOCK : (at + 1) * BLOCK]
                    keep[chunk_slot, first + strip * (STRIP // BLOCK) + at] = block
            return carry

        chunk_slot = chunk
        lax.fori_loop(0, part // STRIP, add, 0)
        if not last:
            continue
        done[chunk] += 1
        if done[chunk] < PARTS:
            continue

        def place(slot, carry, chunk=chunk):
            staged[slot, columns(chunk), :] = keep[chunk, from_ref[slot]] * used_ref[slot]
            return carry

        lax.fori_loop(0, low_count * CAP, place, 0)
        own_slots = pl.ds(me * CAP, CAP)
        for shift in range(1, low_count):
            to = lax.rem(me + shift, low_count)
            copy = pltpu.make_async_remote_copy(
                src_ref=staged.at[pl.ds(to * CAP, CAP), columns(chunk)],
                dst_ref=sketch_ref.at[own_slots, columns(chunk)],
                send_sem=out_sem.at[shift - 1, chunk],
                recv_sem=in_sem.at[shift - 1, chunk],
                device_id={"ry": to},
                device_id_type=pl.DeviceIdType.MESH,
            )
            copy.start()
            arrivals.append(copy)
        sketch_ref[own_slots, columns(chunk), :] = staged[own_slots, columns(chunk), :]
    for copy in arrivals:
        copy.wait()
    for copy in waits:
        copy.wait_send()


def exchange(sizes, x, from_block, used):
    block_count, col_count, _ = x.shape
    row_count = block_count * BLOCK
    chunks = col_count // SUB
    slots = sizes["ry"] * CAP
    bit_count = len(bits_of(sizes))
    vmem = pl.BlockSpec(memory_space=pltpu.VMEM)
    smem = pl.BlockSpec(memory_space=pltpu.SMEM)
    return pl.pallas_call(
        functools.partial(exchange_kernel, sizes),
        out_shape=(
            jax.ShapeDtypeStruct((col_count, row_count), jnp.float32),
            jax.ShapeDtypeStruct((slots, col_count, BLOCK), jnp.float32),
        ),
        in_specs=[smem, smem, vmem],
        out_specs=(vmem, vmem),
        scratch_shapes=[
            pltpu.VMEM((bit_count, col_count, row_count), jnp.float32),
            pltpu.VMEM((slots, col_count, BLOCK), jnp.float32),
            pltpu.VMEM((chunks, row_count // BLOCK, SUB, BLOCK), jnp.float32),
            pltpu.VMEM((col_count, row_count), jnp.float32),
            pltpu.SemaphoreType.DMA((bit_count, chunks * PARTS)),
            pltpu.SemaphoreType.DMA((bit_count, chunks * PARTS)),
            pltpu.SemaphoreType.DMA((sizes["ry"] - 1, chunks)),
            pltpu.SemaphoreType.DMA((sizes["ry"] - 1, chunks)),
        ],
        compiler_params=pltpu.CompilerParams(
            collective_id=0, has_side_effects=True, vmem_limit_bytes=56 * 2**20
        ),
        name="exchange",
    )(from_block, used, x)


def reduce_columns(work):
    tiles, col_count, _ = work.shape
    lane = lax.broadcasted_iota(jnp.int32, (1, LANES), 1)
    for low in range(0, col_count, SUB):
        rest = slice(low, col_count)

        def reflect(column, carry, low=low, rest=rest):
            at = pl.ds(column, 1)
            here = lane == column
            below = jnp.where(lane >= column, work[0, at, :], 0.0)
            top = work[0, rest, :]
            square = below * below
            product = top * below
            for tile in range(1, tiles):
                vector = work[tile, at, :]
                square = square + vector * vector
                product = product + work[tile, rest, :] * vector
            norm2 = jnp.sum(square, axis=1, keepdims=True)
            head = jnp.sum(jnp.where(here, below, 0.0), axis=1, keepdims=True)
            across = jnp.sum(jnp.where(here, top, 0.0), axis=1, keepdims=True)
            product = jnp.sum(product, axis=1, keepdims=True)
            norm = jnp.sqrt(norm2)
            alpha = jnp.where(head >= 0, -norm, norm)
            half = norm2 + jnp.abs(head) * norm
            coef = jnp.where(half > 0, 1.0 / jnp.where(half > 0, half, 1.0), 0.0)
            project = coef * (product - alpha * across)
            first = below - jnp.where(here, alpha, 0.0)
            vectors = [first] + [work[tile, at, :] for tile in range(1, tiles)]
            for tile in range(tiles):
                work[tile, rest, :] = work[tile, rest, :] - project * vectors[tile]
            return carry

        lax.fori_loop(low, low + SUB, reflect, 0)
    square = work[0]
    row_id = lax.broadcasted_iota(jnp.int32, (col_count, LANES), 0)
    lane_id = lax.broadcasted_iota(jnp.int32, (col_count, LANES), 1)
    upper = jnp.where(lane_id <= row_id, square, 0.0)
    diagonal = jnp.sum(jnp.where(lane_id == row_id, upper, 0.0), axis=0, keepdims=True)
    return upper * jnp.where(diagonal >= 0, 1.0, -1.0)


def leaf_kernel(sketch_ref, leaf_ref, work):
    work[...] = sketch_ref[...]
    factor = reduce_columns(work)
    half = factor.shape[0] // 2
    lane = lax.broadcasted_iota(jnp.int32, (half, LANES), 1)
    leaf_ref[...] = jnp.where(lane < LANES // 2, factor[:half], pltpu.roll(factor[half:], LANES // 2, 1))


def leaf(sketch):
    _, col_count, _ = sketch.shape
    return pl.pallas_call(
        leaf_kernel,
        out_shape=jax.ShapeDtypeStruct((col_count // 2, LANES), jnp.float32),
        in_specs=[pl.BlockSpec(memory_space=pltpu.VMEM)],
        out_specs=pl.BlockSpec(memory_space=pltpu.VMEM),
        scratch_shapes=[pltpu.VMEM(sketch.shape, jnp.float32)],
        compiler_params=pltpu.CompilerParams(vmem_limit_bytes=16 * 2**20),
        name="leaf",
    )(sketch)


def gather_kernel(sizes, leaf_ref, all_ref, send_sem, recv_sem, near_send, near_recv):
    low_count = sizes["ry"]
    bits = [bit for bit in bits_of(sizes) if bit[0] == "rx"]
    me = lax.axis_index("ry")
    barrier = pltpu.get_barrier_semaphore()
    for bit in bits:
        pl.semaphore_signal(barrier, inc=1, device_id={"rx": partner_of(*bit)},
                            device_id_type=pl.DeviceIdType.MESH)
    for shift in range(1, low_count):
        pl.semaphore_signal(barrier, inc=1, device_id={"ry": lax.rem(me + shift, low_count)},
                            device_id_type=pl.DeviceIdType.MESH)
    pl.semaphore_wait(barrier, len(bits) + low_count - 1)
    group = 0
    for level, bit in enumerate(bits):
        group = group + 2**level * own_bit(*bit)
    place = pl.ds(group * low_count + me, 1)
    all_ref[place] = leaf_ref[...][None]
    copies = []
    for shift in range(1, low_count):
        copy = pltpu.make_async_remote_copy(
            src_ref=all_ref.at[place], dst_ref=all_ref.at[place],
            send_sem=near_send.at[shift - 1], recv_sem=near_recv.at[shift - 1],
            device_id={"ry": lax.rem(me + shift, low_count)},
            device_id_type=pl.DeviceIdType.MESH,
        )
        copy.start()
        copies.append(copy)
    for copy in copies:
        copy.wait()
    for level, bit in enumerate(bits):
        width = 2**level
        held = all_ref.at[pl.ds(group // width * width * low_count, width * low_count)]
        copy = pltpu.make_async_remote_copy(
            src_ref=held, dst_ref=held,
            send_sem=send_sem.at[level], recv_sem=recv_sem.at[level],
            device_id={"rx": partner_of(*bit)}, device_id_type=pl.DeviceIdType.MESH,
        )
        copy.start()
        copy.wait()


def gather(sizes, leaf_factor):
    bit_count = len(bits_of(sizes))
    return pl.pallas_call(
        functools.partial(gather_kernel, sizes),
        out_shape=jax.ShapeDtypeStruct((sizes["rx"] * sizes["ry"],) + leaf_factor.shape, jnp.float32),
        in_specs=[pl.BlockSpec(memory_space=pltpu.VMEM)],
        out_specs=pl.BlockSpec(memory_space=pltpu.VMEM),
        scratch_shapes=[
            pltpu.SemaphoreType.DMA((bit_count,)),
            pltpu.SemaphoreType.DMA((bit_count,)),
            pltpu.SemaphoreType.DMA((sizes["ry"] - 1,)),
            pltpu.SemaphoreType.DMA((sizes["ry"] - 1,)),
        ],
        compiler_params=pltpu.CompilerParams(collective_id=1, has_side_effects=True),
        name="gather",
    )(leaf_factor)


def final_kernel(scale, all_ref, lower_ref, inverse_ref, work):
    leaves, half, _ = all_ref.shape
    col_count = 2 * half
    lane = lax.broadcasted_iota(jnp.int32, (half, LANES), 1)
    left = lane < LANES // 2
    for tile in range(leaves // 2):
        one, two = all_ref[2 * tile], all_ref[2 * tile + 1]
        work[tile, :half, :] = jnp.where(left, one, pltpu.roll(two, LANES // 2, 1))
        work[tile, half:, :] = jnp.where(left, pltpu.roll(one, LANES // 2, 1), two)
    lower = reduce_columns(work) / scale
    lower_ref[...] = lower
    row_id = lax.broadcasted_iota(jnp.int32, (SUB, LANES), 0)
    lane_id = lax.broadcasted_iota(jnp.int32, (SUB, LANES), 1)
    parts = [
        jnp.where(lane_id == row_id + SUB * part, 1.0, 0.0) for part in range(col_count // SUB)
    ]
    for row in range(col_count):
        part, at = divmod(row, SUB)
        solved = parts[part][at : at + 1, :] / lower[row : row + 1, row : row + 1]
        for later in range(part, col_count // SUB):
            factor = lower[later * SUB : (later + 1) * SUB, row : row + 1]
            reduced = parts[later] - factor * solved
            if later == part:
                reduced = jnp.where(
                    row_id == at, solved, jnp.where(row_id > at, reduced, parts[later])
                )
            parts[later] = reduced
    for part in range(col_count // SUB):
        inverse_ref[part * SUB : (part + 1) * SUB, :] = parts[part]


def final(all_leaves, scale):
    leaves, half, _ = all_leaves.shape
    col_count = 2 * half
    shape = jax.ShapeDtypeStruct((col_count, LANES), jnp.float32)
    vmem = pl.BlockSpec(memory_space=pltpu.VMEM)
    return pl.pallas_call(
        functools.partial(final_kernel, scale),
        out_shape=(shape, shape),
        in_specs=[vmem],
        out_specs=(vmem, vmem),
        scratch_shapes=[pltpu.VMEM((leaves // 2, col_count, LANES), jnp.float32)],
        compiler_params=pltpu.CompilerParams(vmem_limit_bytes=16 * 2**20),
        name="final",
    )(all_leaves)


def slot_sources(pick_ids, owner_ids, slot_count):
    order_ids = jnp.arange(owner_ids.shape[0], dtype=jnp.int32)
    earlier = jnp.logical_and(
        owner_ids[:, None] == owner_ids[None, :], order_ids[None, :] < order_ids[:, None]
    )
    rank_slot = jnp.sum(earlier.astype(jnp.int32), axis=1)
    slot_index = owner_ids * CAP + rank_slot
    match = (jnp.arange(slot_count, dtype=jnp.int32)[:, None] == slot_index[None, :]).astype(jnp.int32)
    return jnp.sum(match * pick_ids[None, :], axis=1), jnp.sum(match, axis=1).astype(jnp.float32)


def per_device(sizes, panel, signs, sample_block, sample_owner):
    col_count, row_count = panel.shape
    block_rows = row_count // LANES
    device_count = sizes["ry"] * sizes["rx"]
    from_block, used = slot_sources(sample_block, sample_owner[:, 0], sizes["ry"] * CAP)
    signed = panel * signs.astype(jnp.float32)[None, :]
    blocked = signed.reshape(col_count, block_rows, LANES)
    blocked = jnp.einsum("cab,bk->cak", blocked, hadamard(LANES), precision=PRECISE)
    blocked = jnp.einsum("cab,ak->kcb", blocked, hadamard(block_rows), precision=PRECISE)
    local = blocked * (1.0 / math.sqrt(row_count * device_count))
    mixed, sketch = exchange(sizes, local, from_block, used)
    received = jnp.transpose(sketch, (1, 0, 2))
    all_leaves = gather(sizes, leaf(sketch))
    lower, inverse = final(all_leaves, math.sqrt(K * BLOCK * device_count))
    r_factor = lower[:, :col_count].T
    solved = jnp.dot(inverse[:, :col_count], panel, precision=PRECISE)
    leverage = jnp.sum(solved * solved, axis=0) / col_count
    return (mixed, received, r_factor, leverage)


def solution(mesh):
    sizes = {name: int(mesh.shape[name]) for name in ("rx", "ry")}
    in_specs = (P(None, ("rx", "ry")), P(("rx", "ry")), P(("rx", "ry")), P(("rx", "ry"), None))
    out_specs = (P(None, ("rx", "ry")), P(None, ("rx", "ry"), None), P(), P(("rx", "ry")))
    return jax.shard_map(
        functools.partial(per_device, sizes), mesh=mesh, in_specs=in_specs, out_specs=out_specs,
        check_vma=False,
    )
```
